32 devices in a mesh: kvh: 4 (over z), blk: 8 (over y, x, core).
Axes of the slice: x: 2, y: 2, z: 4, core: 2. Of those that a mesh axis runs over, the one named last changes fastest.
Arguments:
- queries: bfloat16 [1024, 4096], P('blk', 'kvh')
- suffix_key_rows: bfloat16 [1024, 1024], P('blk', 'kvh')
- suffix_value_rows: bfloat16 [1024, 1024], P('blk', 'kvh'), may hold values from -6 to 6
- prefix_block_keys: bfloat16 [128, 128, 1024], P('blk', None, 'kvh')
- prefix_block_values: bfloat16 [128, 128, 1024], P('blk', None, 'kvh'), may hold values from -6 to 6
- block_group: int32 [128], P('blk'), may hold values from 0 to 3, as said below
- suffix_len: int32 [16], replicated, may hold values from 32 to 96, as said below
- request_group: int32 [16], replicated, may hold values from 0 to 3, as said below
- w_out: bfloat16 [4096, 4096], P('kvh'), may hold values from -1.5 to 1.5
Outputs:
- output: bfloat16 [1024, 4096], P('blk', 'kvh')
The draws below stay inside these ranges and needn't reach their ends.
Inputs may be any that keep to these rules, and one draw needn't show every extreme that they name: `block_group`: every group owns exactly 32 blocks; no index of blk holds more than 4 blocks of one group, and some holds exactly 4. `request_group`: every group has exactly 4 requests. `suffix_len`: the lengths sum to 1024; both ends of the range are reached; no request begins at a multiple of 128 other than 0.
All inputs are finite; a program needn't handle non-finite values.
Results may differ from the reference program's by a relative error of at most 0.005.
Values may be sent and summed in bfloat16 or wider, within the bound.
A program may use at most 256 MiB of HBM per device.

```python
import math
import jax
import jax.numpy as jnp
from jax import lax

D = 4096
QUERY_HEADS = 32
KEY_VALUE_HEADS = 8
HEAD_SIZE = 128
ROWS_PER_SHARD = 128
PREFIX_TOKENS = 4096
BLOCK_TOKENS = 128
SUFFIX_ROWS = 1024
REQ = 16
GROUPS = 4
PREFIX_BLOCKS = 128


def build_query_rows(key):
    random_seed_key = jax.random.fold_in(key, 21)
    unscaled_values = jnp.clip(jax.random.normal(random_seed_key, (SUFFIX_ROWS, QUERY_HEADS * HEAD_SIZE), jnp.float32), -6.0, 6.0)
    return unscaled_values


def draw_queries(key, part):
    return build_query_rows(key).astype(jnp.bfloat16)


def draw_suffix_key_rows(key, part):
    query_head_split = build_query_rows(key).reshape(SUFFIX_ROWS, KEY_VALUE_HEADS, QUERY_HEADS // KEY_VALUE_HEADS, HEAD_SIZE)
    random_noise_term = jnp.clip(jax.random.normal(jax.random.fold_in(key, 31), (SUFFIX_ROWS, KEY_VALUE_HEADS, HEAD_SIZE), jnp.float32), -6.0, 6.0)
    correlated_term = 0.5 * jnp.sum(query_head_split, axis=2) + 0.4 * random_noise_term
    return jnp.clip(correlated_term, -8.0, 8.0).reshape(SUFFIX_ROWS, KEY_VALUE_HEADS * HEAD_SIZE).astype(jnp.bfloat16)


def draw_prefix_block_keys(key, part):
    random_seed_key = jax.random.fold_in(key, 41)
    unscaled_values = jnp.clip(jax.random.normal(random_seed_key, (PREFIX_BLOCKS, BLOCK_TOKENS, KEY_VALUE_HEADS * HEAD_SIZE), jnp.float32), -6.0, 6.0)
    return unscaled_values.astype(jnp.bfloat16)


def draw_block_group(key, part):
    per_group = PREFIX_TOKENS // BLOCK_TOKENS
    holders = 2 * GROUPS
    per_holder = PREFIX_BLOCKS // holders
    places = jnp.arange(PREFIX_BLOCKS, dtype=jnp.int32)
    relabel = jax.random.permutation(jax.random.fold_in(key, 51), GROUPS).astype(jnp.int32)
    rotate = jax.random.randint(jax.random.fold_in(key, 52), (), 0, holders).astype(jnp.int32)
    group_of = relabel[places // per_group]
    holder = (places + rotate) % holders
    local_at = places // holders
    holder_keys = jax.random.split(jax.random.fold_in(key, 53), holders)
    shuffles = jax.vmap(lambda one_key: jax.random.permutation(one_key, per_holder))(holder_keys).astype(jnp.int32)
    target = holder * per_holder + shuffles[holder, local_at]
    return jnp.zeros((PREFIX_BLOCKS,), jnp.int32).at[target].set(group_of).astype(jnp.int32)


def draw_suffix_len(key, part):
    shard_rows = ROWS_PER_SHARD
    pair_count = REQ // 2
    lowest = max(1, shard_rows // 8)
    highest = max(lowest, shard_rows // 4)
    after = jax.random.randint(jax.random.fold_in(key, 71), (pair_count,), lowest, highest + 1).astype(jnp.int32)
    after = after.at[0].set(shard_rows // 4).at[pair_count - 1].set(shard_rows // 4).at[1].set(lowest)
    before = jax.random.randint(jax.random.fold_in(key, 72), (pair_count,), lowest, highest + 1).astype(jnp.int32)
    before = before.at[0].set(0).at[2].set(lowest)
    before_next = jnp.concatenate([before[1:], jnp.zeros((1,), jnp.int32)])
    even_len = before + after
    odd_len = shard_rows - before_next - after
    return jnp.stack([even_len, odd_len], axis=1).reshape(REQ).astype(jnp.int32)


def draw_request_group(key, part):
    return (jax.random.permutation(jax.random.fold_in(key, 61), REQ) // 4).astype(jnp.int32)


def shard_levels(stream_key, dims, shards, low, largest):
    def one(position, parts):
        draws = jax.random.uniform(jax.random.fold_in(jax.random.fold_in(stream_key, 6), position), (parts,), jnp.float32, low / len(shards), largest / len(shards))
        return jnp.repeat(jnp.exp(draws), dims[position] // parts).reshape((-1,) + (1,) * (len(dims) - position - 1))

    level = one(*shards[0])
    for cut in shards[1:]:
        level = level * one(*cut)
    return level


def normal_values(stream_key, dims, width, reach, shards=(), held_as=jnp.bfloat16):
    entries = width * jax.random.normal(stream_key, dims, jnp.float32)
    if shards:
        entries = entries * shard_levels(stream_key, dims, shards, -0.22, 0.18)
    return jnp.clip(entries, -reach, reach).astype(held_as)


def setup_inputs(seed: int = 0) -> dict:
    key_of = jax.random.split(jax.random.key(seed), 10)
    return {
        "queries": draw_queries(jax.random.fold_in(key_of[9], 71), 0),
        "suffix_key_rows": draw_suffix_key_rows(jax.random.fold_in(key_of[9], 71), 0),
        "suffix_value_rows": normal_values(key_of[2], (SUFFIX_ROWS, KEY_VALUE_HEADS * HEAD_SIZE), 1.0, 6.0, ((0, 8), (1, 4))),
        "prefix_block_keys": draw_prefix_block_keys(jax.random.fold_in(key_of[9], 71), 0),
        "prefix_block_values": normal_values(key_of[4], (PREFIX_BLOCKS, BLOCK_TOKENS, KEY_VALUE_HEADS * HEAD_SIZE), 1.0, 6.0, ((0, 8), (2, 4))),
        "block_group": draw_block_group(jax.random.fold_in(key_of[9], 71), 0),
        "suffix_len": draw_suffix_len(jax.random.fold_in(key_of[9], 71), 0),
        "request_group": draw_request_group(jax.random.fold_in(key_of[9], 71), 0),
        "w_out": normal_values(key_of[8], (QUERY_HEADS * HEAD_SIZE, D), (QUERY_HEADS * HEAD_SIZE // 256) ** -0.5, 1.5, ((0, 4),)),
    }


def slot_table(suffix_len, request_group, tok_dev, row_count):
    req_count = suffix_len.shape[0]
    group_count = req_count // 4
    row_ends = jnp.cumsum(suffix_len).astype(jnp.int32)
    starts = (row_ends - suffix_len).astype(jnp.int32)
    member = (request_group[None, :] == jnp.arange(group_count, dtype=jnp.int32)[:, None]).astype(jnp.int32)
    rank_of = (jnp.cumsum(member, axis=1) - 1).astype(jnp.int32)
    slot_ids = jnp.arange(4 * tok_dev, dtype=jnp.int32)
    which_req = slot_ids // tok_dev
    offset = slot_ids % tok_dev
    picked = member[:, None, :] * (rank_of[:, None, :] == which_req[None, :, None]).astype(jnp.int32)
    length = lax.optimization_barrier(jnp.sum(picked * suffix_len[None, None, :], axis=2)).astype(jnp.int32)
    row_begin = lax.optimization_barrier(jnp.sum(picked * starts[None, None, :], axis=2)).astype(jnp.int32)
    slot_valid = offset[None, :] < length
    return (jnp.where(slot_valid, row_begin + offset[None, :], row_count).astype(jnp.int32), slot_valid)

def reference(queries, suffix_key_rows, suffix_value_rows, prefix_block_keys, prefix_block_values, block_group, suffix_len, request_group, w_out):
    row_count = queries.shape[0]
    group_count = suffix_len.shape[0] // 4
    per_group = PREFIX_TOKENS // BLOCK_TOKENS
    query_group_width = QUERY_HEADS // KEY_VALUE_HEADS
    score_scale = 1.0 / math.sqrt(HEAD_SIZE)
    slot_rows, slot_valid = slot_table(suffix_len, request_group, ROWS_PER_SHARD, row_count)
    block_order = jnp.argsort(block_group, stable=True).astype(jnp.int32).reshape(group_count, per_group)
    padded_query_rows = jnp.concatenate([queries, jnp.zeros((1, QUERY_HEADS * HEAD_SIZE), jnp.bfloat16)], axis=0)
    padded_key_rows = jnp.concatenate([suffix_key_rows, jnp.zeros((1, KEY_VALUE_HEADS * HEAD_SIZE), jnp.bfloat16)], axis=0)
    padded_value_rows = jnp.concatenate([suffix_value_rows, jnp.zeros((1, KEY_VALUE_HEADS * HEAD_SIZE), jnp.bfloat16)], axis=0)
    item_rows = slot_rows.reshape(group_count * 4, ROWS_PER_SHARD)
    item_valid = slot_valid.reshape(group_count * 4, ROWS_PER_SHARD)
    item_group = (jnp.arange(group_count * 4, dtype=jnp.int32) // 4).astype(jnp.int32)
    offsets = jnp.arange(ROWS_PER_SHARD, dtype=jnp.int32)
    causal = offsets[None, :] <= offsets[:, None]

    def one_item(packed):
        local_row_count, valid_here, group_here = packed
        local_block_count = block_order[group_here]
        query_float_rows = padded_query_rows[local_row_count].astype(jnp.float32).reshape(ROWS_PER_SHARD, KEY_VALUE_HEADS, query_group_width, HEAD_SIZE)
        prefix_key_rows = prefix_block_keys[local_block_count].astype(jnp.float32).reshape(PREFIX_TOKENS, KEY_VALUE_HEADS, HEAD_SIZE)
        prefix_value_rows = prefix_block_values[local_block_count].astype(jnp.float32).reshape(PREFIX_TOKENS, KEY_VALUE_HEADS, HEAD_SIZE)
        request_key_rows = padded_key_rows[local_row_count].astype(jnp.float32).reshape(ROWS_PER_SHARD, KEY_VALUE_HEADS, HEAD_SIZE)
        request_value_rows = padded_value_rows[local_row_count].astype(jnp.float32).reshape(ROWS_PER_SHARD, KEY_VALUE_HEADS, HEAD_SIZE)
        far_s = jnp.einsum('sgjd,tgd->sgjt', query_float_rows, prefix_key_rows) * score_scale
        near_s = jnp.einsum('sgjd,tgd->sgjt', query_float_rows, request_key_rows) * score_scale
        allowed = causal & valid_here[None, :]
        near_s = jnp.where(allowed[:, None, None, :], near_s, -jnp.inf)
        row_top = jnp.maximum(lax.optimization_barrier(jnp.max(far_s, axis=3)), lax.optimization_barrier(jnp.max(near_s, axis=3)))[..., None]
        far_p = jnp.exp(far_s - row_top)
        near_p = jnp.exp(near_s - row_top)
        denominator = lax.optimization_barrier(jnp.sum(far_p, axis=3)) + lax.optimization_barrier(jnp.sum(near_p, axis=3))
        far_w = lax.optimization_barrier(far_p.astype(jnp.bfloat16)).astype(jnp.float32)
        near_w = lax.optimization_barrier(near_p.astype(jnp.bfloat16)).astype(jnp.float32)
        context = jnp.einsum('sgjt,tgd->sgjd', far_w, prefix_value_rows) + jnp.einsum('sgjt,tgd->sgjd', near_w, request_value_rows)
        return (context / denominator[..., None]).astype(jnp.bfloat16).reshape(ROWS_PER_SHARD, QUERY_HEADS * HEAD_SIZE)
    results = lax.map(one_item, (item_rows, item_valid, item_group))
    attention = jnp.zeros((row_count + 1, QUERY_HEADS * HEAD_SIZE), jnp.bfloat16).at[slot_rows.reshape(-1)].set(results.reshape(-1, QUERY_HEADS * HEAD_SIZE))[:row_count]
    return jnp.dot(attention, w_out, preferred_element_type=jnp.float32).astype(jnp.bfloat16)
```

```python
import functools
import math

import jax
import jax.numpy as jnp
from jax import lax
from jax.experimental import pallas as pl
from jax.experimental.pallas import tpu as pltpu
from jax.sharding import PartitionSpec as P

HEAD_SIZE = 128
SUB = 32
MESH = pl.DeviceIdType.MESH
BF = jnp.bfloat16
F32 = jnp.float32


def dot_t(a, b):
    return lax.dot_general(a, b, (((1,), (1,)), ((), ())), preferred_element_type=F32)


def kernel(
    chips,
    depth,
    len_ref,
    group_ref,
    owner_ref,
    q_ref,
    sk_ref,
    sv_ref,
    k_hbm,
    v_hbm,
    w_hbm,
    out_ref,
    edge_tab,
    first_tab,
    last_tab,
    block_tab,
    k_ref,
    v_ref,
    w_ref,
    pk_ref,
    pv_ref,
    q_same,
    q_other,
    o_same,
    o_other,
    o_back,
    o_pair,
    o_home,
    near_o,
    l_same,
    l_work,
    l_other,
    l_back,
    l_pair,
    l_home,
    near_l,
    att_ref,
    z_out,
    z_in,
    load_sem,
    near_sem,
    q_sem,
    f_sem,
    u_sem,
    c_sem,
    z_sem,
):
    z = lax.axis_index("kvh")
    b = lax.axis_index("blk")
    chip = b // 2
    core = b % 2
    other = 1 - core
    sibling = chip * 2 + other
    blk_count = chips * 2
    tok, q_cols = q_ref.shape
    kv = sk_ref.shape[1] // HEAD_SIZE
    heads = q_cols // HEAD_SIZE
    width = heads // kv
    reqs = len_ref.shape[0]
    groups = reqs // 4
    blocks = k_ref.shape[0]
    subs = tok // SUB
    c2 = math.log2(math.e) / math.sqrt(HEAD_SIZE)

    loads = [
        pltpu.make_async_copy(k_hbm, k_ref, load_sem.at[0]),
        pltpu.make_async_copy(v_hbm, v_ref, load_sem.at[1]),
        pltpu.make_async_copy(w_hbm, w_ref, load_sem.at[2]),
    ]
    for load in loads:
        load.start()

    barrier = pltpu.get_barrier_semaphore()

    def greet(z_to, b_to):
        pl.semaphore_signal(barrier, inc=1, device_id=(z_to, b_to), device_id_type=MESH)

    greet(z, sibling)
    for k in range(1, chips):
        greet(z, lax.rem(chip + k, chips) * 2 + core)
    for d in range(1, depth):
        greet(lax.rem(z + d, depth), b)
    greet(z, lax.rem(b + blk_count - 1, blk_count))

    @pl.loop(0, groups)
    def _(g):
        per = blocks // groups
        rank = jnp.int32(0)
        found = [jnp.int32(0)] * per
        for i in range(blocks):
            hit = owner_ref[i] == g
            found = [
                jnp.where(jnp.logical_and(hit, rank == j), i, found[j]) for j in range(per)
            ]
            rank = rank + jnp.where(hit, 1, 0)
        for j in range(per):
            block_tab[g * per + j] = found[j]

    @pl.loop(0, blk_count * subs)
    def _(s):
        row = s * SUB
        start = jnp.int32(0)
        edge = first = last = jnp.int32(0)
        for r in range(reqs):
            end = start + len_ref[r]
            group = group_ref[r]
            here = start <= row
            edge = jnp.where(here, end, edge)
            first = jnp.where(here, group, first)
            last = jnp.where(start <= row + (SUB - 1), group, last)
            start = end
        edge_tab[s] = edge - row
        first_tab[s] = first
        last_tab[s] = last

    pl.semaphore_wait(barrier, chips + depth)

    def remote(src, dst, send, recv, b_to, z_to=None):
        return pltpu.make_async_remote_copy(
            src_ref=src,
            dst_ref=dst,
            send_sem=send,
            recv_sem=recv,
            device_id=(z if z_to is None else z_to, b_to),
            device_id_type=MESH,
        )

    def q_copy(k):
        return remote(
            q_ref,
            q_same.at[k],
            q_sem.at[0, k],
            q_sem.at[1, k],
            lax.rem(chip + k, chips) * 2 + core,
        )

    def f_copy(k, src):
        return remote(src, q_other.at[k], f_sem.at[0, k], f_sem.at[1, k], sibling)

    def u_copies(k):
        return (
            remote(o_other.at[k], o_back.at[k], u_sem.at[0, k], u_sem.at[1, k], sibling),
            remote(l_other.at[k], l_back.at[k], u_sem.at[2, k], u_sem.at[3, k], sibling),
        )

    def c_copies(k):
        to = lax.rem(chip + chips - k, chips) * 2 + core
        return (
            remote(o_pair.at[k], o_home.at[k], c_sem.at[0, k], c_sem.at[1, k], to),
            remote(l_pair.at[k], l_home.at[k], c_sem.at[2, k], c_sem.at[3, k], to),
        )

    f_copy(0, q_ref).start()
    for k in range(1, chips):
        q_copy(k).start()
    after = lax.rem(b + 1, blk_count)
    near_copies = (
        remote(sk_ref, pk_ref, near_sem.at[0], near_sem.at[1], after),
        remote(sv_ref, pv_ref, near_sem.at[2], near_sem.at[3], after),
    )
    for copy in near_copies:
        copy.start()
    loads[0].wait()
    loads[1].wait()

    lane = lax.broadcasted_iota(jnp.int32, (SUB, HEAD_SIZE), 1)
    sub_row = lax.broadcasted_iota(jnp.int32, (SUB, HEAD_SIZE), 0)
    per = blocks // groups

    def attend(q_in, tile, o_out, l_out):
        @pl.loop(0, subs)
        def _(i):
            s = tile * subs + i
            rows = pl.ds(pl.multiple_of(i * SUB, SUB), SUB)
            q = q_in[rows, :]
            upper = jnp.where(sub_row < edge_tab[s], 1.0, 0.0)
            upper = jnp.concatenate([upper] * width, axis=0)
            upper16 = upper.astype(BF)
            a_blocks = [block_tab[first_tab[s] * per + j] for j in range(per)]
            b_blocks = [block_tab[last_tab[s] * per + j] for j in range(per)]
            stat = jnp.zeros((SUB, HEAD_SIZE), F32)
            for g in range(kv):
                cols = slice(g * HEAD_SIZE, (g + 1) * HEAD_SIZE)
                qs = jnp.concatenate(
                    [
                        q[:, (g * width + j) * HEAD_SIZE : (g * width + j + 1) * HEAD_SIZE]
                        for j in range(width)
                    ],
                    axis=0,
                )
                qa = qs * upper16
                both = jnp.concatenate([qa, qs - qa], axis=1)
                keys = jnp.concatenate(
                    [
                        jnp.concatenate([k_ref[x][:, cols], k_ref[y][:, cols]], axis=1)
                        for x, y in zip(a_blocks, b_blocks)
                    ],
                    axis=0,
                )
                values = jnp.concatenate(
                    [
                        jnp.concatenate([v_ref[x][:, cols], v_ref[y][:, cols]], axis=1)
                        for x, y in zip(a_blocks, b_blocks)
                    ],
                    axis=0,
                )
                scores = dot_t(both, keys)
                top = jnp.max(scores, axis=1, keepdims=True) * c2
                prob = jnp.exp2(scores * c2 - top)
                total = jnp.sum(prob, axis=1, keepdims=True)
                mixed = jnp.dot(prob.astype(BF), values, preferred_element_type=F32)
                context = jnp.where(upper > 0.5, mixed[:, :HEAD_SIZE], mixed[:, HEAD_SIZE:])
                context = (context * (1.0 / total)).astype(BF)
                level = top + jnp.log2(total)
                for j in range(width):
                    h = g * width + j
                    part = slice(j * SUB, (j + 1) * SUB)
                    o_out[rows, h * HEAD_SIZE : (h + 1) * HEAD_SIZE] = context[part]
                    stat = jnp.where(lane == h, level[part], stat)
            l_out[rows, :] = stat

    def thin(stat):
        return jnp.transpose(stat)[:heads]

    def wide(flat):
        return jnp.transpose(jnp.concatenate([flat] * (HEAD_SIZE // heads), axis=0))

    def attend_other(k, q_in):
        tile = lax.rem(chip + chips - k, chips) * 2 + other
        attend(q_in, tile, o_other.at[k], l_work)
        l_other[k] = thin(l_work[...])
        for copy in u_copies(k):
            copy.start()

    def attend_same(k, q_in):
        tile = lax.rem(chip + chips - k, chips) * 2 + core
        attend(q_in, tile, o_same.at[k], l_same.at[k])

    def pair(k, o_out, l_out):
        for copy in u_copies(k):
            copy.wait_recv()
        la = l_same[k]
        lb = wide(l_back[k])
        top = jnp.maximum(la, lb)
        wa = jnp.exp2(la - top)
        wb = jnp.exp2(lb - top)
        total = wa + wb
        l_out[...] = thin(top + jnp.log2(total))
        wa = wa / total
        wb = wb / total
        for h in range(heads):
            cols = slice(h * HEAD_SIZE, (h + 1) * HEAD_SIZE)
            o_out[:, cols] = (
                o_same[k, :, cols].astype(F32) * wa[:, h : h + 1]
                + o_back[k, :, cols].astype(F32) * wb[:, h : h + 1]
            ).astype(BF)

    attend_same(0, q_ref)
    f_copy(0, q_ref).wait_recv()
    attend_other(0, q_other.at[0])

    for copy in near_copies:
        copy.wait_recv()
    own_row = b * tok + lax.broadcasted_iota(jnp.int32, (tok, 2 * tok), 0)
    key_row = (b - 1) * tok + lax.broadcasted_iota(jnp.int32, (tok, 2 * tok), 1)
    begin = jnp.zeros((tok, 2 * tok), jnp.int32)
    start = jnp.int32(0)
    for r in range(reqs):
        begin = jnp.where(own_row >= start, start, begin)
        start = start + len_ref[r]
    bias = jnp.where(
        jnp.logical_and(key_row >= begin, key_row <= own_row), 0.0, -jnp.inf
    )
    wide_lane = lax.broadcasted_iota(jnp.int32, (tok, HEAD_SIZE), 1)
    stat = jnp.zeros((tok, HEAD_SIZE), F32)
    for g in range(kv):
        cols = slice(g * HEAD_SIZE, (g + 1) * HEAD_SIZE)
        keys = jnp.concatenate([pk_ref[:, cols], sk_ref[:, cols]], axis=0)
        values = jnp.concatenate([pv_ref[:, cols], sv_ref[:, cols]], axis=0)
        for j in range(width):
            h = g * width + j
            hc = slice(h * HEAD_SIZE, (h + 1) * HEAD_SIZE)
            scores = dot_t(q_ref[:, hc], keys) * c2 + bias
            top = jnp.max(scores, axis=1, keepdims=True)
            prob = jnp.exp2(scores - top)
            total = jnp.sum(prob, axis=1, keepdims=True)
            context = jnp.dot(prob.astype(BF), values, preferred_element_type=F32)
            near_o[:, hc] = context * (1.0 / total)
            stat = jnp.where(wide_lane == h, top + jnp.log2(total), stat)
    near_l[...] = stat

    @pl.loop(1, chips)
    def _(k):
        q_copy(k).wait_recv()
        f_copy(k, q_same.at[k]).start()
        attend_same(k, q_same.at[k])

        @pl.when(k == 1)
        def _():
            pair(0, o_home.at[0], l_home.at[0])

        @pl.when(k > 1)
        def _():
            pair(k - 1, o_pair.at[k - 1], l_pair.at[k - 1])
            for copy in c_copies(k - 1):
                copy.start()

        f_copy(k, q_same.at[k]).wait_recv()
        attend_other(k, q_other.at[k])

    pair(chips - 1, o_pair.at[chips - 1], l_pair.at[chips - 1])
    for copy in c_copies(chips - 1):
        copy.start()

    for k in range(1, chips):
        for copy in c_copies(k):
            copy.wait_recv()
    levels = [wide(l_home[k]) for k in range(chips)]
    top = near_l[...]
    for level in levels:
        top = jnp.maximum(top, level)
    near_w = jnp.exp2(near_l[...] - top)
    weights = [jnp.exp2(level - top) for level in levels]
    total = near_w
    for weight in weights:
        total = total + weight
    near_w = near_w / total
    weights = [weight / total for weight in weights]
    for h in range(heads):
        cols = slice(h * HEAD_SIZE, (h + 1) * HEAD_SIZE)
        acc = near_o[:, cols] * near_w[:, h : h + 1]
        for k in range(chips):
            acc = acc + o_home[k, :, cols].astype(F32) * weights[k][:, h : h + 1]
        att_ref[:, cols] = acc.astype(BF)

    loads[2].wait()
    out_cols = out_ref.shape[1]
    step = 512 if out_cols % 512 == 0 else out_cols

    def z_copy(d):
        return remote(
            z_out.at[d], z_in.at[d], z_sem.at[0, d], z_sem.at[1, d], b, lax.rem(z + d, depth)
        )

    @pl.loop(1, depth)
    def _(d):
        to = lax.rem(z + d, depth)

        @pl.loop(0, out_cols // step)
        def _(t):
            at = pl.ds(pl.multiple_of(to * out_cols + t * step, step), step)
            z_out[d, :, pl.ds(pl.multiple_of(t * step, step), step)] = jnp.dot(
                att_ref[...], w_ref[:, at], preferred_element_type=F32
            ).astype(BF)

        z_copy(d).start()

    @pl.loop(0, out_cols // step)
    def _(t):
        at = pl.ds(pl.multiple_of(z * out_cols + t * step, step), step)
        near_o[:, pl.ds(pl.multiple_of(t * step, step), step)] = jnp.dot(
            att_ref[...], w_ref[:, at], preferred_element_type=F32
        )

    for d in range(1, depth):
        z_copy(d).wait_recv()
    acc = near_o[...]
    for d in range(1, depth):
        acc = acc + z_in[d].astype(F32)
    out_ref[...] = acc.astype(BF)

    for copy in near_copies:
        copy.wait_send()
    f_copy(0, q_ref).wait_send()
    for copy in u_copies(0):
        copy.wait_send()
    for k in range(1, chips):
        q_copy(k).wait_send()
        f_copy(k, q_same.at[k]).wait_send()
        for copy in u_copies(k):
            copy.wait_send()
        for copy in c_copies(k):
            copy.wait_send()
    for d in range(1, depth):
        z_copy(d).wait_send()


def per_device(
    queries,
    suffix_key_rows,
    suffix_value_rows,
    prefix_block_keys,
    prefix_block_values,
    block_group,
    suffix_len,
    request_group,
    w_out,
):
    tok, q_cols = queries.shape
    kv_cols = suffix_key_rows.shape[1]
    heads = q_cols // HEAD_SIZE
    blk_count = lax.axis_size("blk")
    depth = lax.axis_size("kvh")
    chips = blk_count // 2
    blocks = prefix_block_keys.shape[0]
    out_cols = w_out.shape[1] // depth
    subs = blk_count * tok // SUB
    smem = pl.BlockSpec(memory_space=pltpu.SMEM)
    vmem = pl.BlockSpec(memory_space=pltpu.VMEM)
    hbm = pl.BlockSpec(memory_space=pl.ANY)
    tiles = pltpu.VMEM((chips, tok, q_cols), BF)
    thin = pltpu.VMEM((chips, heads, tok), F32)
    dma = pltpu.SemaphoreType.DMA
    return pl.pallas_call(
        functools.partial(kernel, chips, depth),
        out_shape=jax.ShapeDtypeStruct((tok, out_cols), BF),
        in_specs=[smem] * 3 + [vmem] * 3 + [hbm] * 3,
        out_specs=vmem,
        scratch_shapes=[
            pltpu.SMEM((subs,), jnp.int32),
            pltpu.SMEM((subs,), jnp.int32),
            pltpu.SMEM((subs,), jnp.int32),
            pltpu.SMEM((blocks,), jnp.int32),
            pltpu.VMEM(prefix_block_keys.shape, BF),
            pltpu.VMEM(prefix_block_values.shape, BF),
            pltpu.VMEM(w_out.shape, BF),
            pltpu.VMEM((tok, kv_cols), BF),
            pltpu.VMEM((tok, kv_cols), BF),
            tiles,
            tiles,
            tiles,
            tiles,
            tiles,
            tiles,
            tiles,
            pltpu.VMEM((tok, q_cols), F32),
            pltpu.VMEM((chips, tok, HEAD_SIZE), F32),
            pltpu.VMEM((tok, HEAD_SIZE), F32),
            thin,
            thin,
            thin,
            thin,
            pltpu.VMEM((tok, HEAD_SIZE), F32),
            pltpu.VMEM((tok, q_cols), BF),
            pltpu.VMEM((depth, tok, out_cols), BF),
            pltpu.VMEM((depth, tok, out_cols), BF),
            dma((3,)),
            dma((4,)),
            dma((2, chips)),
            dma((2, chips)),
            dma((4, chips)),
            dma((4, chips)),
            dma((2, depth)),
        ],
        compiler_params=pltpu.CompilerParams(
            collective_id=0, has_side_effects=True, vmem_limit_bytes=56 * 1024 * 1024
        ),
    )(
        suffix_len,
        request_group,
        block_group,
        queries,
        suffix_key_rows,
        suffix_value_rows,
        prefix_block_keys,
        prefix_block_values,
        w_out,
    )


def solution(mesh):
    placed = (
        P("blk", "kvh"),
        P("blk", "kvh"),
        P("blk", "kvh"),
        P("blk", None, "kvh"),
        P("blk", None, "kvh"),
        P("blk"),
        P(),
        P(),
        P("kvh", None),
    )
    return jax.shard_map(
        per_device, mesh=mesh, in_specs=placed, out_specs=P("blk", "kvh"), check_vma=False
    )
```

```python
import functools
import math

import jax
import jax.numpy as jnp
from jax import lax
from jax.experimental import pallas as pl
from jax.experimental.pallas import tpu as pltpu
from jax.sharding import PartitionSpec as P

HEAD_SIZE = 128
SUB = 32
CHUNKS = 2
MESH = pl.DeviceIdType.MESH
BF = jnp.bfloat16
F32 = jnp.float32


def dot_t(a, b):
    return lax.dot_general(a, b, (((1,), (1,)), ((), ())), preferred_element_type=F32)


def kernel(
    chips,
    depth,
    len_ref,
    group_ref,
    owner_ref,
    q_ref,
    sk_ref,
    sv_ref,
    k_hbm,
    v_hbm,
    w_hbm,
    out_ref,
    edge_tab,
    first_tab,
    last_tab,
    block_tab,
    k_ref,
    v_ref,
    w_ref,
    pk_ref,
    pv_ref,
    q_same,
    q_other,
    o_same,
    o_other,
    o_back,
    o_pair,
    o_home,
    near_o,
    l_same,
    l_work,
    l_other,
    l_back,
    l_pair,
    l_home,
    near_l,
    att_ref,
    z_out,
    z_in,
    load_sem,
    near_sem,
    q_sem,
    f_sem,
    u_sem,
    c_sem,
    z_sem,
):
    z = lax.axis_index("kvh")
    b = lax.axis_index("blk")
    chip = b // 2
    core = b % 2
    other = 1 - core
    sibling = chip * 2 + other
    blk_count = chips * 2
    tok, q_cols = q_ref.shape
    kv = sk_ref.shape[1] // HEAD_SIZE
    heads = q_cols // HEAD_SIZE
    width = heads // kv
    reqs = len_ref.shape[0]
    groups = reqs // 4
    blocks = k_ref.shape[0]
    subs = tok // SUB
    part_subs = subs // CHUNKS
    size = tok // CHUNKS
    c2 = math.log2(math.e) / math.sqrt(HEAD_SIZE)

    loads = [
        pltpu.make_async_copy(k_hbm, k_ref, load_sem.at[0]),
        pltpu.make_async_copy(v_hbm, v_ref, load_sem.at[1]),
        pltpu.make_async_copy(w_hbm, w_ref, load_sem.at[2]),
    ]
    for load in loads:
        load.start()

    barrier = pltpu.get_barrier_semaphore()

    def greet(z_to, b_to):
        pl.semaphore_signal(barrier, inc=1, device_id=(z_to, b_to), device_id_type=MESH)

    greet(z, sibling)
    for k in range(1, chips):
        greet(z, lax.rem(chip + k, chips) * 2 + core)
    for d in range(1, depth):
        greet(lax.rem(z + d, depth), b)
    greet(z, lax.rem(b + blk_count - 1, blk_count))

    @pl.loop(0, groups)
    def _(g):
        per = blocks // groups
        rank = jnp.int32(0)
        found = [jnp.int32(0)] * per
        for i in range(blocks):
            hit = owner_ref[i] == g
            found = [
                jnp.where(jnp.logical_and(hit, rank == j), i, found[j]) for j in range(per)
            ]
            rank = rank + jnp.where(hit, 1, 0)
        for j in range(per):
            block_tab[g * per + j] = found[j]

    @pl.loop(0, blk_count * subs)
    def _(s):
        row = s * SUB
        start = jnp.int32(0)
        edge = first = last = jnp.int32(0)
        for r in range(reqs):
            end = start + len_ref[r]
            group = group_ref[r]
            here = start <= row
            edge = jnp.where(here, end, edge)
            first = jnp.where(here, group, first)
            last = jnp.where(start <= row + (SUB - 1), group, last)
            start = end
        edge_tab[s] = edge - row
        first_tab[s] = first
        last_tab[s] = last

    pl.semaphore_wait(barrier, chips + depth)

    def remote(src, dst, send, recv, b_to, z_to=None):
        return pltpu.make_async_remote_copy(
            src_ref=src,
            dst_ref=dst,
            send_sem=send,
            recv_sem=recv,
            device_id=(z if z_to is None else z_to, b_to),
            device_id_type=MESH,
        )

    def span(c):
        return pl.ds(c * size, size)

    def q_copy(k, c):
        return remote(
            q_ref.at[span(c)],
            q_same.at[k, span(c)],
            q_sem.at[0, k, c],
            q_sem.at[1, k, c],
            lax.rem(chip + k, chips) * 2 + core,
        )

    def f_copy(k, c, src):
        return remote(
            src.at[span(c)],
            q_other.at[k, span(c)],
            f_sem.at[0, k, c],
            f_sem.at[1, k, c],
            sibling,
        )

    def u_copies(k, c):
        return (
            remote(
                o_other.at[k, span(c)],
                o_back.at[k, span(c)],
                u_sem.at[0, k, c],
                u_sem.at[1, k, c],
                sibling,
            ),
            remote(l_other.at[k, c], l_back.at[k, c], u_sem.at[2, k, c], u_sem.at[3, k, c], sibling),
        )

    def c_copies(k, c):
        to = lax.rem(chip + chips - k, chips) * 2 + core
        return (
            remote(
                o_pair.at[k, span(c)],
                o_home.at[k, span(c)],
                c_sem.at[0, k, c],
                c_sem.at[1, k, c],
                to,
            ),
            remote(l_pair.at[k, c], l_home.at[k, c], c_sem.at[2, k, c], c_sem.at[3, k, c], to),
        )

    after = lax.rem(b + 1, blk_count)
    near_copies = (
        remote(sk_ref, pk_ref, near_sem.at[0], near_sem.at[1], after),
        remote(sv_ref, pv_ref, near_sem.at[2], near_sem.at[3], after),
    )
    for c in range(CHUNKS):
        f_copy(0, c, q_ref).start()
        for k in range(1, chips):
            q_copy(k, c).start()
        if c == 0:
            for copy in near_copies:
                copy.start()
    loads[0].wait()
    loads[1].wait()

    lane = lax.broadcasted_iota(jnp.int32, (SUB, HEAD_SIZE), 1)
    sub_row = lax.broadcasted_iota(jnp.int32, (SUB, HEAD_SIZE), 0)
    per = blocks // groups

    def attend(q_in, tile, o_out, l_out, c):
        @pl.loop(c * part_subs, (c + 1) * part_subs, unroll=part_subs)
        def _(i):
            s = tile * subs + i
            rows = pl.ds(pl.multiple_of(i * SUB, SUB), SUB)
            q = q_in[rows, :]
            upper = jnp.where(sub_row < edge_tab[s], 1.0, 0.0)
            upper = jnp.concatenate([upper] * width, axis=0)
            upper16 = upper.astype(BF)
            a_blocks = [block_tab[first_tab[s] * per + j] for j in range(per)]
            b_blocks = [block_tab[last_tab[s] * per + j] for j in range(per)]
            stat = jnp.zeros((SUB, HEAD_SIZE), F32)
            for g in range(kv):
                cols = slice(g * HEAD_SIZE, (g + 1) * HEAD_SIZE)
                qs = jnp.concatenate(
                    [
                        q[:, (g * width + j) * HEAD_SIZE : (g * width + j + 1) * HEAD_SIZE]
                        for j in range(width)
                    ],
                    axis=0,
                )
                qa = qs * upper16
                both = jnp.concatenate([qa, qs - qa], axis=1)
                keys = jnp.concatenate(
                    [
                        jnp.concatenate([k_ref[x][:, cols], k_ref[y][:, cols]], axis=1)
                        for x, y in zip(a_blocks, b_blocks)
                    ],
                    axis=0,
                )
                values = jnp.concatenate(
                    [
                        jnp.concatenate([v_ref[x][:, cols], v_ref[y][:, cols]], axis=1)
                        for x, y in zip(a_blocks, b_blocks)
                    ],
                    axis=0,
                )
                scores = dot_t(both, keys)
                top = jnp.max(scores, axis=1, keepdims=True) * c2
                prob = jnp.exp2(scores * c2 - top)
                total = jnp.sum(prob, axis=1, keepdims=True)
                mixed = jnp.dot(prob.astype(BF), values, preferred_element_type=F32)
                context = jnp.where(upper > 0.5, mixed[:, :HEAD_SIZE], mixed[:, HEAD_SIZE:])
                context = (context * (1.0 / total)).astype(BF)
                level = top + jnp.log2(total)
                for j in range(width):
                    h = g * width + j
                    part = slice(j * SUB, (j + 1) * SUB)
                    o_out[rows, h * HEAD_SIZE : (h + 1) * HEAD_SIZE] = context[part]
                    stat = jnp.where(lane == h, level[part], stat)
            l_out[rows, :] = stat

    def thin(stat):
        return jnp.transpose(jnp.concatenate([stat] * CHUNKS, axis=0))[:heads]

    def wide(flat):
        return jnp.transpose(jnp.concatenate([flat] * (HEAD_SIZE // heads), axis=0))[:size]

    def attend_other(k, q_in, c):
        tile = lax.rem(chip + chips - k, chips) * 2 + other
        attend(q_in, tile, o_other.at[k], l_work, c)
        l_other[k, c] = thin(l_work[span(c), :])
        for copy in u_copies(k, c):
            copy.start()

    def attend_same(k, q_in, c):
        tile = lax.rem(chip + chips - k, chips) * 2 + core
        attend(q_in, tile, o_same.at[k], l_same.at[k], c)

    def pair(k, o_out, l_out, c):
        for copy in u_copies(k, c):
            copy.wait_recv()
        la = l_same[k, span(c), :]
        lb = wide(l_back[k, c])
        top = jnp.maximum(la, lb)
        wa = jnp.exp2(la - top)
        wb = jnp.exp2(lb - top)
        total = wa + wb
        l_out[...] = thin(top + jnp.log2(total))
        wa = wa / total
        wb = wb / total
        for h in range(heads):
            cols = slice(h * HEAD_SIZE, (h + 1) * HEAD_SIZE)
            o_out[span(c), cols] = (
                o_same[k, span(c), cols].astype(F32) * wa[:, h : h + 1]
                + o_back[k, span(c), cols].astype(F32) * wb[:, h : h + 1]
            ).astype(BF)

    def own_chip(c):
        attend_same(0, q_ref, c)
        f_copy(0, c, q_ref).wait_recv()
        attend_other(0, q_other.at[0], c)

    own_chip(0)

    for copy in near_copies:
        copy.wait_recv()
    own_row = b * tok + lax.broadcasted_iota(jnp.int32, (tok, 2 * tok), 0)
    key_row = (b - 1) * tok + lax.broadcasted_iota(jnp.int32, (tok, 2 * tok), 1)
    begin = jnp.zeros((tok, 2 * tok), jnp.int32)
    start = jnp.int32(0)
    for r in range(reqs):
        begin = jnp.where(own_row >= start, start, begin)
        start = start + len_ref[r]
    bias = jnp.where(
        jnp.logical_and(key_row >= begin, key_row <= own_row), 0.0, -jnp.inf
    )
    wide_lane = lax.broadcasted_iota(jnp.int32, (tok, HEAD_SIZE), 1)
    stat = jnp.zeros((tok, HEAD_SIZE), F32)
    for g in range(kv):
        cols = slice(g * HEAD_SIZE, (g + 1) * HEAD_SIZE)
        keys = jnp.concatenate([pk_ref[:, cols], sk_ref[:, cols]], axis=0)
        values = jnp.concatenate([pv_ref[:, cols], sv_ref[:, cols]], axis=0)
        for j in range(width):
            h = g * width + j
            hc = slice(h * HEAD_SIZE, (h + 1) * HEAD_SIZE)
            scores = dot_t(q_ref[:, hc], keys) * c2 + bias
            top = jnp.max(scores, axis=1, keepdims=True)
            prob = jnp.exp2(scores - top)
            total = jnp.sum(prob, axis=1, keepdims=True)
            context = jnp.dot(prob.astype(BF), values, preferred_element_type=F32)
            near_o[:, hc] = context * (1.0 / total)
            stat = jnp.where(wide_lane == h, top + jnp.log2(total), stat)
    near_l[...] = stat

    for c in range(CHUNKS):
        if c > 0:
            own_chip(c)

        @pl.loop(1, chips)
        def _(k):
            q_copy(k, c).wait_recv()
            f_copy(k, c, q_same.at[k]).start()
            attend_same(k, q_same.at[k], c)

            @pl.when(k == 1)
            def _():
                pair(0, o_home.at[0], l_home.at[0, c], c)

            @pl.when(k > 1)
            def _():
                pair(k - 1, o_pair.at[k - 1], l_pair.at[k - 1, c], c)
                for copy in c_copies(k - 1, c):
                    copy.start()

            f_copy(k, c, q_same.at[k]).wait_recv()
            attend_other(k, q_other.at[k], c)

        pair(chips - 1, o_pair.at[chips - 1], l_pair.at[chips - 1, c], c)
        for copy in c_copies(chips - 1, c):
            copy.start()

    loads[2].wait()
    out_cols = out_ref.shape[1]
    step = 512 if out_cols % 512 == 0 else out_cols

    def z_copy(d, c):
        return remote(
            z_out.at[d, span(c)],
            z_in.at[d, span(c)],
            z_sem.at[0, d, c],
            z_sem.at[1, d, c],
            b,
            lax.rem(z + d, depth),
        )

    for c in range(CHUNKS):
        for k in range(1, chips):
            for copy in c_copies(k, c):
                copy.wait_recv()
        levels = [wide(l_home[k, c]) for k in range(chips)]
        near_level = near_l[span(c), :]
        top = near_level
        for level in levels:
            top = jnp.maximum(top, level)
        near_w = jnp.exp2(near_level - top)
        weights = [jnp.exp2(level - top) for level in levels]
        total = near_w
        for weight in weights:
            total = total + weight
        near_w = near_w / total
        weights = [weight / total for weight in weights]
        for h in range(heads):
            cols = slice(h * HEAD_SIZE, (h + 1) * HEAD_SIZE)
            acc = near_o[span(c), cols] * near_w[:, h : h + 1]
            for k in range(chips):
                acc = acc + o_home[k, span(c), cols].astype(F32) * weights[k][:, h : h + 1]
            att_ref[span(c), cols] = acc.astype(BF)

        @pl.loop(1, depth)
        def _(d):
            to = lax.rem(z + d, depth)

            @pl.loop(0, out_cols // step)
            def _(t):
                at = pl.ds(pl.multiple_of(to * out_cols + t * step, step), step)
                z_out[d, span(c), pl.ds(pl.multiple_of(t * step, step), step)] = jnp.dot(
                    att_ref[span(c), :], w_ref[:, at], preferred_element_type=F32
                ).astype(BF)

            z_copy(d, c).start()

    @pl.loop(0, out_cols // step)
    def _(t):
        at = pl.ds(pl.multiple_of(z * out_cols + t * step, step), step)
        near_o[:, pl.ds(pl.multiple_of(t * step, step), step)] = jnp.dot(
            att_ref[...], w_ref[:, at], preferred_element_type=F32
        )

    for c in range(CHUNKS):
        for d in range(1, depth):
            z_copy(d, c).wait_recv()
        acc = near_o[span(c), :]
        for d in range(1, depth):
            acc = acc + z_in[d, span(c), :].astype(F32)
        out_ref[span(c), :] = acc.astype(BF)

    for copy in near_copies:
        copy.wait_send()
    for c in range(CHUNKS):
        f_copy(0, c, q_ref).wait_send()
        for copy in u_copies(0, c):
            copy.wait_send()
        for k in range(1, chips):
            q_copy(k, c).wait_send()
            f_copy(k, c, q_same.at[k]).wait_send()
            for copy in u_copies(k, c):
                copy.wait_send()
            for copy in c_copies(k, c):
                copy.wait_send()
        for d in range(1, depth):
            z_copy(d, c).wait_send()


def per_device(
    queries,
    suffix_key_rows,
    suffix_value_rows,
    prefix_block_keys,
    prefix_block_values,
    block_group,
    suffix_len,
    request_group,
    w_out,
):
    tok, q_cols = queries.shape
    kv_cols = suffix_key_rows.shape[1]
    heads = q_cols // HEAD_SIZE
    blk_count = lax.axis_size("blk")
    depth = lax.axis_size("kvh")
    chips = blk_count // 2
    blocks = prefix_block_keys.shape[0]
    out_cols = w_out.shape[1] // depth
    subs = blk_count * tok // SUB
    smem = pl.BlockSpec(memory_space=pltpu.SMEM)
    vmem = pl.BlockSpec(memory_space=pltpu.VMEM)
    hbm = pl.BlockSpec(memory_space=pl.ANY)
    tiles = pltpu.VMEM((chips, tok, q_cols), BF)
    thin = pltpu.VMEM((chips, CHUNKS, heads, tok), F32)
    dma = pltpu.SemaphoreType.DMA
    return pl.pallas_call(
        functools.partial(kernel, chips, depth),
        out_shape=jax.ShapeDtypeStruct((tok, out_cols), BF),
        in_specs=[smem] * 3 + [vmem] * 3 + [hbm] * 3,
        out_specs=vmem,
        scratch_shapes=[
            pltpu.SMEM((subs,), jnp.int32),
            pltpu.SMEM((subs,), jnp.int32),
            pltpu.SMEM((subs,), jnp.int32),
            pltpu.SMEM((blocks,), jnp.int32),
            pltpu.VMEM(prefix_block_keys.shape, BF),
            pltpu.VMEM(prefix_block_values.shape, BF),
            pltpu.VMEM(w_out.shape, BF),
            pltpu.VMEM((tok, kv_cols), BF),
            pltpu.VMEM((tok, kv_cols), BF),
            tiles,
            tiles,
            tiles,
            tiles,
            tiles,
            tiles,
            tiles,
            pltpu.VMEM((tok, q_cols), F32),
            pltpu.VMEM((chips, tok, HEAD_SIZE), F32),
            pltpu.VMEM((tok, HEAD_SIZE), F32),
            thin,
            thin,
            thin,
            thin,
            pltpu.VMEM((tok, HEAD_SIZE), F32),
            pltpu.VMEM((tok, q_cols), BF),
            pltpu.VMEM((depth, tok, out_cols), BF),
            pltpu.VMEM((depth, tok, out_cols), BF),
            dma((3,)),
            dma((4,)),
            dma((2, chips, CHUNKS)),
            dma((2, chips, CHUNKS)),
            dma((4, chips, CHUNKS)),
            dma((4, chips, CHUNKS)),
            dma((2, depth, CHUNKS)),
        ],
        compiler_params=pltpu.CompilerParams(
            collective_id=0, has_side_effects=True, vmem_limit_bytes=56 * 1024 * 1024
        ),
    )(
        suffix_len,
        request_group,
        block_group,
        queries,
        suffix_key_rows,
        suffix_value_rows,
        prefix_block_keys,
        prefix_block_values,
        w_out,
    )


def solution(mesh):
    placed = (
        P("blk", "kvh"),
        P("blk", "kvh"),
        P("blk", "kvh"),
        P("blk", None, "kvh"),
        P("blk", None, "kvh"),
        P("blk"),
        P(),
        P(),
        P("kvh", None),
    )
    return jax.shard_map(
        per_device, mesh=mesh, in_specs=placed, out_specs=P("blk", "kvh"), check_vma=False
    )
```

```python
import functools
import math

import jax
import jax.numpy as jnp
from jax import lax
from jax.experimental import pallas as pl
from jax.experimental.pallas import tpu as pltpu
from jax.sharding import PartitionSpec as P

HEAD_SIZE = 128
SUB = 32
CHUNKS = 2
MESH = pl.DeviceIdType.MESH
BF = jnp.bfloat16
F32 = jnp.float32


def dot_t(a, b):
    return lax.dot_general(a, b, (((1,), (1,)), ((), ())), preferred_element_type=F32)


def kernel(
    chips,
    depth,
    len_ref,
    group_ref,
    owner_ref,
    q_ref,
    sk_ref,
    sv_ref,
    k_hbm,
    v_hbm,
    w_hbm,
    out_ref,
    edge_tab,
    first_tab,
    last_tab,
    block_tab,
    k_ref,
    v_ref,
    w_ref,
    pk_ref,
    pv_ref,
    q_same,
    q_other,
    o_same,
    o_other,
    o_back,
    o_pair,
    o_home,
    near_o,
    l_same,
    l_work,
    l_other,
    l_back,
    l_pair,
    l_home,
    near_l,
    att_ref,
    z_out,
    z_in,
    load_sem,
    near_sem,
    q_sem,
    f_sem,
    u_sem,
    c_sem,
    z_sem,
):
    z = lax.axis_index("kvh")
    b = lax.axis_index("blk")
    chip = b // 2
    core = b % 2
    other = 1 - core
    sibling = chip * 2 + other
    blk_count = chips * 2
    tok, q_cols = q_ref.shape
    kv = sk_ref.shape[1] // HEAD_SIZE
    heads = q_cols // HEAD_SIZE
    width = heads // kv
    reqs = len_ref.shape[0]
    groups = reqs // 4
    blocks = k_ref.shape[0]
    subs = tok // SUB
    part_subs = subs // CHUNKS
    size = tok // CHUNKS
    c2 = math.log2(math.e) / math.sqrt(HEAD_SIZE)

    loads = [
        pltpu.make_async_copy(k_hbm, k_ref, load_sem.at[0]),
        pltpu.make_async_copy(v_hbm, v_ref, load_sem.at[1]),
        pltpu.make_async_copy(w_hbm, w_ref, load_sem.at[2]),
    ]
    for load in loads:
        load.start()

    barrier = pltpu.get_barrier_semaphore()

    def greet(z_to, b_to):
        pl.semaphore_signal(barrier, inc=1, device_id=(z_to, b_to), device_id_type=MESH)

    greet(z, sibling)
    for k in range(1, chips):
        greet(z, lax.rem(chip + k, chips) * 2 + core)
    for d in range(1, depth):
        greet(lax.rem(z + d, depth), b)
    greet(z, lax.rem(b + blk_count - 1, blk_count))

    @pl.loop(0, groups)
    def _(g):
        per = blocks // groups
        rank = jnp.int32(0)
        found = [jnp.int32(0)] * per
        for i in range(blocks):
            hit = owner_ref[i] == g
            found = [
                jnp.where(jnp.logical_and(hit, rank == j), i, found[j]) for j in range(per)
            ]
            rank = rank + jnp.where(hit, 1, 0)
        for j in range(per):
            block_tab[g * per + j] = found[j]

    @pl.loop(0, blk_count * subs)
    def _(s):
        row = s * SUB
        start = jnp.int32(0)
        edge = first = last = jnp.int32(0)
        for r in range(reqs):
            end = start + len_ref[r]
            group = group_ref[r]
            here = start <= row
            edge = jnp.where(here, end, edge)
            first = jnp.where(here, group, first)
            last = jnp.where(start <= row + (SUB - 1), group, last)
            start = end
        edge_tab[s] = edge - row
        first_tab[s] = first
        last_tab[s] = last

    pl.semaphore_wait(barrier, chips + depth)

    def remote(src, dst, send, recv, b_to, z_to=None):
        return pltpu.make_async_remote_copy(
            src_ref=src,
            dst_ref=dst,
            send_sem=send,
            recv_sem=recv,
            device_id=(z if z_to is None else z_to, b_to),
            device_id_type=MESH,
        )

    def span(c):
        return pl.ds(c * size, size)

    def q_copy(k, c):
        return remote(
            q_ref.at[span(c)],
            q_same.at[k, span(c)],
            q_sem.at[0, k, c],
            q_sem.at[1, k, c],
            lax.rem(chip + k, chips) * 2 + core,
        )

    def f_copy(k, c, src):
        return remote(
            src.at[span(c)],
            q_other.at[k, span(c)],
            f_sem.at[0, k, c],
            f_sem.at[1, k, c],
            sibling,
        )

    def u_copies(k, c):
        return (
            remote(
                o_other.at[k, span(c)],
                o_back.at[k, span(c)],
                u_sem.at[0, k, c],
                u_sem.at[1, k, c],
                sibling,
            ),
            remote(l_other.at[k, c], l_back.at[k, c], u_sem.at[2, k, c], u_sem.at[3, k, c], sibling),
        )

    def c_copies(k, c):
        to = lax.rem(chip + chips - k, chips) * 2 + core
        return (
            remote(
                o_pair.at[k, span(c)],
                o_home.at[k, span(c)],
                c_sem.at[0, k, c],
                c_sem.at[1, k, c],
                to,
            ),
            remote(l_pair.at[k, c], l_home.at[k, c], c_sem.at[2, k, c], c_sem.at[3, k, c], to),
        )

    after = lax.rem(b + 1, blk_count)
    near_copies = (
        remote(sk_ref, pk_ref, near_sem.at[0], near_sem.at[1], after),
        remote(sv_ref, pv_ref, near_sem.at[2], near_sem.at[3], after),
    )
    for c in range(CHUNKS):
        f_copy(0, c, q_ref).start()
        for k in range(1, chips):
            q_copy(k, c).start()
        if c == 0:
            for copy in near_copies:
                copy.start()
    loads[0].wait()
    loads[1].wait()

    lane = lax.broadcasted_iota(jnp.int32, (SUB, HEAD_SIZE), 1)
    sub_row = lax.broadcasted_iota(jnp.int32, (SUB, HEAD_SIZE), 0)
    per = blocks // groups

    def attend(q_in, tile, o_out, l_out, c):
        @pl.loop(c * part_subs, (c + 1) * part_subs, unroll=part_subs)
        def _(i):
            s = tile * subs + i
            rows = pl.ds(pl.multiple_of(i * SUB, SUB), SUB)
            q = q_in[rows, :]
            upper = jnp.where(sub_row < edge_tab[s], 1.0, 0.0)
            upper = jnp.concatenate([upper] * width, axis=0)
            upper16 = upper.astype(BF)
            a_blocks = [block_tab[first_tab[s] * per + j] for j in range(per)]
            b_blocks = [block_tab[last_tab[s] * per + j] for j in range(per)]
            stat = jnp.zeros((SUB, HEAD_SIZE), F32)
            for g in range(kv):
                cols = slice(g * HEAD_SIZE, (g + 1) * HEAD_SIZE)
                qs = jnp.concatenate(
                    [
                        q[:, (g * width + j) * HEAD_SIZE : (g * width + j + 1) * HEAD_SIZE]
                        for j in range(width)
                    ],
                    axis=0,
                )
                qa = qs * upper16
                both = jnp.concatenate([qa, qs - qa], axis=1)
                keys = jnp.concatenate(
                    [
                        jnp.concatenate([k_ref[x][:, cols], k_ref[y][:, cols]], axis=1)
                        for x, y in zip(a_blocks, b_blocks)
                    ],
                    axis=0,
                )
                values = jnp.concatenate(
                    [
                        jnp.concatenate([v_ref[x][:, cols], v_ref[y][:, cols]], axis=1)
                        for x, y in zip(a_blocks, b_blocks)
                    ],
                    axis=0,
                )
                scores = dot_t(both, keys)
                top = jnp.max(scores, axis=1, keepdims=True) * c2
                prob = jnp.exp2(scores * c2 - top)
                total = jnp.sum(prob, axis=1, keepdims=True)
                mixed = jnp.dot(prob.astype(BF), values, preferred_element_type=F32)
                context = jnp.where(upper > 0.5, mixed[:, :HEAD_SIZE], mixed[:, HEAD_SIZE:])
                context = (context * (1.0 / total)).astype(BF)
                level = top + jnp.log2(total)
                for j in range(width):
                    h = g * width + j
                    part = slice(j * SUB, (j + 1) * SUB)
                    o_out[rows, h * HEAD_SIZE : (h + 1) * HEAD_SIZE] = context[part]
                    stat = jnp.where(lane == h, level[part], stat)
            l_out[rows, :] = stat

    def thin(stat):
        return jnp.transpose(jnp.concatenate([stat] * CHUNKS, axis=0))[:heads]

    def wide(flat):
        return jnp.transpose(jnp.concatenate([flat] * (HEAD_SIZE // heads), axis=0))[:size]

    def attend_other(k, q_in, c):
        tile = lax.rem(chip + chips - k, chips) * 2 + other
        attend(q_in, tile, o_other.at[k], l_work, c)
        l_other[k, c] = thin(l_work[span(c), :])
        for copy in u_copies(k, c):
            copy.start()

    def attend_same(k, q_in, c):
        tile = lax.rem(chip + chips - k, chips) * 2 + core
        attend(q_in, tile, o_same.at[k], l_same.at[k], c)

    def pair(k, o_out, l_out, c):
        for copy in u_copies(k, c):
            copy.wait_recv()
        la = l_same[k, span(c), :]
        lb = wide(l_back[k, c])
        top = jnp.maximum(la, lb)
        wa = jnp.exp2(la - top)
        wb = jnp.exp2(lb - top)
        total = wa + wb
        l_out[...] = thin(top + jnp.log2(total))
        wa = wa / total
        wb = wb / total
        for h in range(heads):
            cols = slice(h * HEAD_SIZE, (h + 1) * HEAD_SIZE)
            o_out[span(c), cols] = (
                o_same[k, span(c), cols].astype(F32) * wa[:, h : h + 1]
                + o_back[k, span(c), cols].astype(F32) * wb[:, h : h + 1]
            ).astype(BF)

    def own_chip(c):
        attend_same(0, q_ref, c)
        f_copy(0, c, q_ref).wait_recv()
        attend_other(0, q_other.at[0], c)

    own_chip(0)

    for copy in near_copies:
        copy.wait_recv()
    own_row = b * tok + lax.broadcasted_iota(jnp.int32, (tok, 2 * tok), 0)
    key_row = (b - 1) * tok + lax.broadcasted_iota(jnp.int32, (tok, 2 * tok), 1)
    begin = jnp.zeros((tok, 2 * tok), jnp.int32)
    start = jnp.int32(0)
    for r in range(reqs):
        begin = jnp.where(own_row >= start, start, begin)
        start = start + len_ref[r]
    bias = jnp.where(
        jnp.logical_and(key_row >= begin, key_row <= own_row), 0.0, -jnp.inf
    )
    wide_lane = lax.broadcasted_iota(jnp.int32, (tok, HEAD_SIZE), 1)
    stat = jnp.zeros((tok, HEAD_SIZE), F32)
    for g in range(kv):
        cols = slice(g * HEAD_SIZE, (g + 1) * HEAD_SIZE)
        keys = jnp.concatenate([pk_ref[:, cols], sk_ref[:, cols]], axis=0)
        values = jnp.concatenate([pv_ref[:, cols], sv_ref[:, cols]], axis=0)
        for j in range(width):
            h = g * width + j
            hc = slice(h * HEAD_SIZE, (h + 1) * HEAD_SIZE)
            scores = dot_t(q_ref[:, hc], keys) * c2 + bias
            top = jnp.max(scores, axis=1, keepdims=True)
            prob = jnp.exp2(scores - top)
            total = jnp.sum(prob, axis=1, keepdims=True)
            context = jnp.dot(prob.astype(BF), values, preferred_element_type=F32)
            near_o[:, hc] = context * (1.0 / total)
            stat = jnp.where(wide_lane == h, top + jnp.log2(total), stat)
    near_l[...] = stat

    loads[2].wait()
    out_cols = out_ref.shape[1]
    step = 512 if out_cols % 512 == 0 else out_cols

    def z_copy(d, c):
        return remote(
            z_out.at[d, span(c)],
            z_in.at[d, span(c)],
            z_sem.at[0, d, c],
            z_sem.at[1, d, c],
            b,
            lax.rem(z + d, depth),
        )

    def finish(c):
        for k in range(1, chips):
            for copy in c_copies(k, c):
                copy.wait_recv()
        levels = [wide(l_home[k, c]) for k in range(chips)]
        near_level = near_l[span(c), :]
        top = near_level
        for level in levels:
            top = jnp.maximum(top, level)
        near_w = jnp.exp2(near_level - top)
        weights = [jnp.exp2(level - top) for level in levels]
        total = near_w
        for weight in weights:
            total = total + weight
        near_w = near_w / total
        weights = [weight / total for weight in weights]
        for h in range(heads):
            cols = slice(h * HEAD_SIZE, (h + 1) * HEAD_SIZE)
            acc = near_o[span(c), cols] * near_w[:, h : h + 1]
            for k in range(chips):
                acc = acc + o_home[k, span(c), cols].astype(F32) * weights[k][:, h : h + 1]
            att_ref[span(c), cols] = acc.astype(BF)

        @pl.loop(1, depth)
        def _(d):
            to = lax.rem(z + d, depth)

            @pl.loop(0, out_cols // step)
            def _(t):
                at = pl.ds(pl.multiple_of(to * out_cols + t * step, step), step)
                z_out[d, span(c), pl.ds(pl.multiple_of(t * step, step), step)] = jnp.dot(
                    att_ref[span(c), :], w_ref[:, at], preferred_element_type=F32
                ).astype(BF)

            z_copy(d, c).start()

    for c in range(CHUNKS):
        if c > 0:
            own_chip(c)

        @pl.loop(1, chips)
        def _(k):
            if c > 0:
                pl.when(k == chips // 2)(lambda: finish(c - 1))

            q_copy(k, c).wait_recv()
            f_copy(k, c, q_same.at[k]).start()
            attend_same(k, q_same.at[k], c)

            @pl.when(k == 1)
            def _():
                pair(0, o_home.at[0], l_home.at[0, c], c)

            @pl.when(k > 1)
            def _():
                pair(k - 1, o_pair.at[k - 1], l_pair.at[k - 1, c], c)
                for copy in c_copies(k - 1, c):
                    copy.start()

            f_copy(k, c, q_same.at[k]).wait_recv()
            attend_other(k, q_other.at[k], c)

        pair(chips - 1, o_pair.at[chips - 1], l_pair.at[chips - 1, c], c)
        for copy in c_copies(chips - 1, c):
            copy.start()

    finish(CHUNKS - 1)

    @pl.loop(0, out_cols // step)
    def _(t):
        at = pl.ds(pl.multiple_of(z * out_cols + t * step, step), step)
        near_o[:, pl.ds(pl.multiple_of(t * step, step), step)] = jnp.dot(
            att_ref[...], w_ref[:, at], preferred_element_type=F32
        )

    for c in range(CHUNKS):
        for d in range(1, depth):
            z_copy(d, c).wait_recv()
        acc = near_o[span(c), :]
        for d in range(1, depth):
            acc = acc + z_in[d, span(c), :].astype(F32)
        out_ref[span(c), :] = acc.astype(BF)

    for copy in near_copies:
        copy.wait_send()
    for c in range(CHUNKS):
        f_copy(0, c, q_ref).wait_send()
        for copy in u_copies(0, c):
            copy.wait_send()
        for k in range(1, chips):
            q_copy(k, c).wait_send()
            f_copy(k, c, q_same.at[k]).wait_send()
            for copy in u_copies(k, c):
                copy.wait_send()
            for copy in c_copies(k, c):
                copy.wait_send()
        for d in range(1, depth):
            z_copy(d, c).wait_send()


def per_device(
    queries,
    suffix_key_rows,
    suffix_value_rows,
    prefix_block_keys,
    prefix_block_values,
    block_group,
    suffix_len,
    request_group,
    w_out,
):
    tok, q_cols = queries.shape
    kv_cols = suffix_key_rows.shape[1]
    heads = q_cols // HEAD_SIZE
    blk_count = lax.axis_size("blk")
    depth = lax.axis_size("kvh")
    chips = blk_count // 2
    blocks = prefix_block_keys.shape[0]
    out_cols = w_out.shape[1] // depth
    subs = blk_count * tok // SUB
    smem = pl.BlockSpec(memory_space=pltpu.SMEM)
    vmem = pl.BlockSpec(memory_space=pltpu.VMEM)
    hbm = pl.BlockSpec(memory_space=pl.ANY)
    tiles = pltpu.VMEM((chips, tok, q_cols), BF)
    thin = pltpu.VMEM((chips, CHUNKS, heads, tok), F32)
    dma = pltpu.SemaphoreType.DMA
    return pl.pallas_call(
        functools.partial(kernel, chips, depth),
        out_shape=jax.ShapeDtypeStruct((tok, out_cols), BF),
        in_specs=[smem] * 3 + [vmem] * 3 + [hbm] * 3,
        out_specs=vmem,
        scratch_shapes=[
            pltpu.SMEM((subs,), jnp.int32),
            pltpu.SMEM((subs,), jnp.int32),
            pltpu.SMEM((subs,), jnp.int32),
            pltpu.SMEM((blocks,), jnp.int32),
            pltpu.VMEM(prefix_block_keys.shape, BF),
            pltpu.VMEM(prefix_block_values.shape, BF),
            pltpu.VMEM(w_out.shape, BF),
            pltpu.VMEM((tok, kv_cols), BF),
            pltpu.VMEM((tok, kv_cols), BF),
            tiles,
            tiles,
            tiles,
            tiles,
            tiles,
            tiles,
            tiles,
            pltpu.VMEM((tok, q_cols), F32),
            pltpu.VMEM((chips, tok, HEAD_SIZE), F32),
            pltpu.VMEM((tok, HEAD_SIZE), F32),
            thin,
            thin,
            thin,
            thin,
            pltpu.VMEM((tok, HEAD_SIZE), F32),
            pltpu.VMEM((tok, q_cols), BF),
            pltpu.VMEM((depth, tok, out_cols), BF),
            pltpu.VMEM((depth, tok, out_cols), BF),
            dma((3,)),
            dma((4,)),
            dma((2, chips, CHUNKS)),
            dma((2, chips, CHUNKS)),
            dma((4, chips, CHUNKS)),
            dma((4, chips, CHUNKS)),
            dma((2, depth, CHUNKS)),
        ],
        compiler_params=pltpu.CompilerParams(
            collective_id=0, has_side_effects=True, vmem_limit_bytes=56 * 1024 * 1024
        ),
    )(
        suffix_len,
        request_group,
        block_group,
        queries,
        suffix_key_rows,
        suffix_value_rows,
        prefix_block_keys,
        prefix_block_values,
        w_out,
    )


def solution(mesh):
    placed = (
        P("blk", "kvh"),
        P("blk", "kvh"),
        P("blk", "kvh"),
        P("blk", None, "kvh"),
        P("blk", None, "kvh"),
        P("blk"),
        P(),
        P(),
        P("kvh", None),
    )
    return jax.shard_map(
        per_device, mesh=mesh, in_specs=placed, out_specs=P("blk", "kvh"), check_vma=False
    )
```

```python
import functools
import math

import jax
import jax.numpy as jnp
from jax import lax
from jax.experimental import pallas as pl
from jax.experimental.pallas import tpu as pltpu
from jax.sharding import PartitionSpec as P

HEAD_SIZE = 128
SUB = 32
CHUNKS = 2
MESH = pl.DeviceIdType.MESH
BF = jnp.bfloat16
F32 = jnp.float32


def dot_t(a, b):
    return lax.dot_general(a, b, (((1,), (1,)), ((), ())), preferred_element_type=F32)


def kernel(
    chips,
    depth,
    len_ref,
    group_ref,
    owner_ref,
    q_ref,
    sk_ref,
    sv_ref,
    k_hbm,
    v_hbm,
    w_hbm,
    out_ref,
    edge_tab,
    first_tab,
    last_tab,
    block_tab,
    k_ref,
    v_ref,
    w_ref,
    pk_ref,
    pv_ref,
    q_same,
    q_other,
    o_same,
    o_other,
    o_back,
    o_pair,
    o_home,
    near_o,
    l_same,
    l_work,
    l_other,
    l_back,
    l_pair,
    l_home,
    near_l,
    att_ref,
    z_out,
    z_in,
    load_sem,
    near_sem,
    q_sem,
    f_sem,
    u_sem,
    c_sem,
    z_sem,
):
    z = lax.axis_index("kvh")
    b = lax.axis_index("blk")
    chip = b // 2
    core = b % 2
    other = 1 - core
    sibling = chip * 2 + other
    blk_count = chips * 2
    tok, q_cols = q_ref.shape
    kv = sk_ref.shape[1] // HEAD_SIZE
    heads = q_cols // HEAD_SIZE
    width = heads // kv
    reqs = len_ref.shape[0]
    groups = reqs // 4
    blocks = k_ref.shape[0]
    subs = tok // SUB
    part_subs = subs // CHUNKS
    size = tok // CHUNKS
    c2 = math.log2(math.e) / math.sqrt(HEAD_SIZE)

    loads = [
        pltpu.make_async_copy(k_hbm, k_ref, load_sem.at[0]),
        pltpu.make_async_copy(v_hbm, v_ref, load_sem.at[1]),
        pltpu.make_async_copy(w_hbm, w_ref, load_sem.at[2]),
    ]
    for load in loads:
        load.start()

    barrier = pltpu.get_barrier_semaphore()

    def greet(z_to, b_to):
        pl.semaphore_signal(barrier, inc=1, device_id=(z_to, b_to), device_id_type=MESH)

    greet(z, sibling)
    for k in range(1, chips):
        greet(z, lax.rem(chip + k, chips) * 2 + core)
    for d in range(1, depth):
        greet(lax.rem(z + d, depth), b)
    greet(z, lax.rem(b + blk_count - 1, blk_count))

    @pl.loop(0, groups)
    def _(g):
        per = blocks // groups
        rank = jnp.int32(0)
        found = [jnp.int32(0)] * per
        for i in range(blocks):
            hit = owner_ref[i] == g
            found = [
                jnp.where(jnp.logical_and(hit, rank == j), i, found[j]) for j in range(per)
            ]
            rank = rank + jnp.where(hit, 1, 0)
        for j in range(per):
            block_tab[g * per + j] = found[j]

    @pl.loop(0, blk_count * subs)
    def _(s):
        row = s * SUB
        start = jnp.int32(0)
        edge = first = last = jnp.int32(0)
        for r in range(reqs):
            end = start + len_ref[r]
            group = group_ref[r]
            here = start <= row
            edge = jnp.where(here, end, edge)
            first = jnp.where(here, group, first)
            last = jnp.where(start <= row + (SUB - 1), group, last)
            start = end
        edge_tab[s] = edge - row
        first_tab[s] = first
        last_tab[s] = last

    pl.semaphore_wait(barrier, chips + depth)

    def remote(src, dst, send, recv, b_to, z_to=None):
        return pltpu.make_async_remote_copy(
            src_ref=src,
            dst_ref=dst,
            send_sem=send,
            recv_sem=recv,
            device_id=(z if z_to is None else z_to, b_to),
            device_id_type=MESH,
        )

    def span(c):
        return pl.ds(c * size, size)

    def q_copy(k, c):
        return remote(
            q_ref.at[span(c)],
            q_same.at[k, span(c)],
            q_sem.at[0, k, c],
            q_sem.at[1, k, c],
            lax.rem(chip + k, chips) * 2 + core,
        )

    def f_copy(k, c, src):
        return remote(
            src.at[span(c)],
            q_other.at[k, span(c)],
            f_sem.at[0, k, c],
            f_sem.at[1, k, c],
            sibling,
        )

    def u_copies(k, c):
        return (
            remote(
                o_other.at[k, span(c)],
                o_back.at[k, span(c)],
                u_sem.at[0, k, c],
                u_sem.at[1, k, c],
                sibling,
            ),
            remote(l_other.at[k, c], l_back.at[k, c], u_sem.at[2, k, c], u_sem.at[3, k, c], sibling),
        )

    def c_copies(k, c):
        to = lax.rem(chip + chips - k, chips) * 2 + core
        return (
            remote(
                o_pair.at[k, span(c)],
                o_home.at[k, span(c)],
                c_sem.at[0, k, c],
                c_sem.at[1, k, c],
                to,
            ),
            remote(l_pair.at[k, c], l_home.at[k, c], c_sem.at[2, k, c], c_sem.at[3, k, c], to),
        )

    after = lax.rem(b + 1, blk_count)
    near_copies = (
        remote(sk_ref, pk_ref, near_sem.at[0], near_sem.at[1], after),
        remote(sv_ref, pv_ref, near_sem.at[2], near_sem.at[3], after),
    )
    for c in range(CHUNKS):
        f_copy(0, c, q_ref).start()
        for k in range(1, chips):
            q_copy(k, c).start()
        if c == 0:
            for copy in near_copies:
                copy.start()
    loads[0].wait()
    loads[1].wait()

    lane = lax.broadcasted_iota(jnp.int32, (SUB, HEAD_SIZE), 1)
    sub_row = lax.broadcasted_iota(jnp.int32, (SUB, HEAD_SIZE), 0)
    per = blocks // groups

    def attend(q_in, tile, o_out, l_out, c):
        @pl.loop(c * part_subs, (c + 1) * part_subs, unroll=part_subs)
        def _(i):
            s = tile * subs + i
            rows = pl.ds(pl.multiple_of(i * SUB, SUB), SUB)
            q = q_in[rows, :]
            upper = jnp.where(sub_row < edge_tab[s], 1.0, 0.0)
            upper = jnp.concatenate([upper] * width, axis=0)
            upper16 = upper.astype(BF)
            a_blocks = [block_tab[first_tab[s] * per + j] for j in range(per)]
            b_blocks = [block_tab[last_tab[s] * per + j] for j in range(per)]
            stat = jnp.zeros((SUB, HEAD_SIZE), F32)
            for g in range(kv):
                cols = slice(g * HEAD_SIZE, (g + 1) * HEAD_SIZE)
                qs = jnp.concatenate(
                    [
                        q[:, (g * width + j) * HEAD_SIZE : (g * width + j + 1) * HEAD_SIZE]
                        for j in range(width)
                    ],
                    axis=0,
                )
                qa = qs * upper16
                both = jnp.concatenate([qa, qs - qa], axis=1)
                keys = jnp.concatenate(
                    [
                        jnp.concatenate([k_ref[x][:, cols], k_ref[y][:, cols]], axis=1)
                        for x, y in zip(a_blocks, b_blocks)
                    ],
                    axis=0,
                )
                values = jnp.concatenate(
                    [
                        jnp.concatenate([v_ref[x][:, cols], v_ref[y][:, cols]], axis=1)
                        for x, y in zip(a_blocks, b_blocks)
                    ],
                    axis=0,
                )
                scores = dot_t(both, keys)
                top = jnp.max(scores, axis=1, keepdims=True) * c2
                prob = jnp.exp2(scores * c2 - top)
                total = jnp.sum(prob, axis=1, keepdims=True)
                mixed = jnp.dot(prob.astype(BF), values, preferred_element_type=F32)
                context = jnp.where(upper > 0.5, mixed[:, :HEAD_SIZE], mixed[:, HEAD_SIZE:])
                context = (context * (1.0 / total)).astype(BF)
                level = top + jnp.log2(total)
                for j in range(width):
                    h = g * width + j
                    part = slice(j * SUB, (j + 1) * SUB)
                    o_out[rows, h * HEAD_SIZE : (h + 1) * HEAD_SIZE] = context[part]
                    stat = jnp.where(lane == h, level[part], stat)
            l_out[rows, :] = stat

    def thin(stat):
        return jnp.transpose(jnp.concatenate([stat] * CHUNKS, axis=0))[:heads]

    def wide(flat):
        return jnp.transpose(jnp.concatenate([flat] * (HEAD_SIZE // heads), axis=0))[:size]

    def attend_other(k, q_in, c):
        tile = lax.rem(chip + chips - k, chips) * 2 + other
        attend(q_in, tile, o_other.at[k], l_work, c)
        l_other[k, c] = thin(l_work[span(c), :])
        for copy in u_copies(k, c):
            copy.start()

    def attend_same(k, q_in, c):
        tile = lax.rem(chip + chips - k, chips) * 2 + core
        attend(q_in, tile, o_same.at[k], l_same.at[k], c)

    def pair(k, o_out, l_out, c):
        for copy in u_copies(k, c):
            copy.wait_recv()
        la = l_same[k, span(c), :]
        lb = wide(l_back[k, c])
        top = jnp.maximum(la, lb)
        wa = jnp.exp2(la - top)
        wb = jnp.exp2(lb - top)
        total = wa + wb
        l_out[...] = thin(top + jnp.log2(total))
        wa = wa / total
        wb = wb / total
        for h in range(heads):
            cols = slice(h * HEAD_SIZE, (h + 1) * HEAD_SIZE)
            o_out[span(c), cols] = (
                o_same[k, span(c), cols].astype(F32) * wa[:, h : h + 1]
                + o_back[k, span(c), cols].astype(F32) * wb[:, h : h + 1]
            ).astype(BF)

    def own_chip(c):
        attend_same(0, q_ref, c)
        f_copy(0, c, q_ref).wait_recv()
        attend_other(0, q_other.at[0], c)

    def near():
        for copy in near_copies:
            copy.wait_recv()
        own_row = b * tok + lax.broadcasted_iota(jnp.int32, (tok, 2 * tok), 0)
        key_row = (b - 1) * tok + lax.broadcasted_iota(jnp.int32, (tok, 2 * tok), 1)
        begin = jnp.zeros((tok, 2 * tok), jnp.int32)
        start = jnp.int32(0)
        for r in range(reqs):
            begin = jnp.where(own_row >= start, start, begin)
            start = start + len_ref[r]
        bias = jnp.where(
            jnp.logical_and(key_row >= begin, key_row <= own_row), 0.0, -jnp.inf
        )
        wide_lane = lax.broadcasted_iota(jnp.int32, (tok, HEAD_SIZE), 1)
        stat = jnp.zeros((tok, HEAD_SIZE), F32)
        for g in range(kv):
            cols = slice(g * HEAD_SIZE, (g + 1) * HEAD_SIZE)
            keys = jnp.concatenate([pk_ref[:, cols], sk_ref[:, cols]], axis=0)
            values = jnp.concatenate([pv_ref[:, cols], sv_ref[:, cols]], axis=0)
            for j in range(width):
                h = g * width + j
                hc = slice(h * HEAD_SIZE, (h + 1) * HEAD_SIZE)
                scores = dot_t(q_ref[:, hc], keys) * c2 + bias
                top = jnp.max(scores, axis=1, keepdims=True)
                prob = jnp.exp2(scores - top)
                total = jnp.sum(prob, axis=1, keepdims=True)
                context = jnp.dot(prob.astype(BF), values, preferred_element_type=F32)
                near_o[:, hc] = context * (1.0 / total)
                stat = jnp.where(wide_lane == h, top + jnp.log2(total), stat)
        near_l[...] = stat

    own_chip(0)


    loads[2].wait()
    out_cols = out_ref.shape[1]
    step = 512 if out_cols % 512 == 0 else out_cols

    def z_copy(d, c):
        return remote(
            z_out.at[d, span(c)],
            z_in.at[d, span(c)],
            z_sem.at[0, d, c],
            z_sem.at[1, d, c],
            b,
            lax.rem(z + d, depth),
        )

    def finish(c):
        for k in range(1, chips):
            for copy in c_copies(k, c):
                copy.wait_recv()
        levels = [wide(l_home[k, c]) for k in range(chips)]
        near_level = near_l[span(c), :]
        top = near_level
        for level in levels:
            top = jnp.maximum(top, level)
        near_w = jnp.exp2(near_level - top)
        weights = [jnp.exp2(level - top) for level in levels]
        total = near_w
        for weight in weights:
            total = total + weight
        near_w = near_w / total
        weights = [weight / total for weight in weights]
        for h in range(heads):
            cols = slice(h * HEAD_SIZE, (h + 1) * HEAD_SIZE)
            acc = near_o[span(c), cols] * near_w[:, h : h + 1]
            for k in range(chips):
                acc = acc + o_home[k, span(c), cols].astype(F32) * weights[k][:, h : h + 1]
            att_ref[span(c), cols] = acc.astype(BF)

        @pl.loop(1, depth)
        def _(d):
            to = lax.rem(z + d, depth)

            @pl.loop(0, out_cols // step)
            def _(t):
                at = pl.ds(pl.multiple_of(to * out_cols + t * step, step), step)
                z_out[d, span(c), pl.ds(pl.multiple_of(t * step, step), step)] = jnp.dot(
                    att_ref[span(c), :], w_ref[:, at], preferred_element_type=F32
                ).astype(BF)

            z_copy(d, c).start()

    for c in range(CHUNKS):
        if c > 0:
            own_chip(c)
        if c == 1:
            near()

        @pl.loop(1, chips)
        def _(k):
            if c > 0:
                pl.when(k == chips // 2)(lambda: finish(c - 1))

            q_copy(k, c).wait_recv()
            f_copy(k, c, q_same.at[k]).start()
            attend_same(k, q_same.at[k], c)

            @pl.when(k == 1)
            def _():
                pair(0, o_home.at[0], l_home.at[0, c], c)

            @pl.when(k > 1)
            def _():
                pair(k - 1, o_pair.at[k - 1], l_pair.at[k - 1, c], c)
                for copy in c_copies(k - 1, c):
                    copy.start()

            f_copy(k, c, q_same.at[k]).wait_recv()
            attend_other(k, q_other.at[k], c)

        pair(chips - 1, o_pair.at[chips - 1], l_pair.at[chips - 1, c], c)
        for copy in c_copies(chips - 1, c):
            copy.start()

    finish(CHUNKS - 1)

    @pl.loop(0, out_cols // step)
    def _(t):
        at = pl.ds(pl.multiple_of(z * out_cols + t * step, step), step)
        near_o[:, pl.ds(pl.multiple_of(t * step, step), step)] = jnp.dot(
            att_ref[...], w_ref[:, at], preferred_element_type=F32
        )

    for c in range(CHUNKS):
        for d in range(1, depth):
            z_copy(d, c).wait_recv()
        acc = near_o[span(c), :]
        for d in range(1, depth):
            acc = acc + z_in[d, span(c), :].astype(F32)
        out_ref[span(c), :] = acc.astype(BF)

    for copy in near_copies:
        copy.wait_send()
    for c in range(CHUNKS):
        f_copy(0, c, q_ref).wait_send()
        for copy in u_copies(0, c):
            copy.wait_send()
        for k in range(1, chips):
            q_copy(k, c).wait_send()
            f_copy(k, c, q_same.at[k]).wait_send()
            for copy in u_copies(k, c):
                copy.wait_send()
            for copy in c_copies(k, c):
                copy.wait_send()
        for d in range(1, depth):
            z_copy(d, c).wait_send()


def per_device(
    queries,
    suffix_key_rows,
    suffix_value_rows,
    prefix_block_keys,
    prefix_block_values,
    block_group,
    suffix_len,
    request_group,
    w_out,
):
    tok, q_cols = queries.shape
    kv_cols = suffix_key_rows.shape[1]
    heads = q_cols // HEAD_SIZE
    blk_count = lax.axis_size("blk")
    depth = lax.axis_size("kvh")
    chips = blk_count // 2
    blocks = prefix_block_keys.shape[0]
    out_cols = w_out.shape[1] // depth
    subs = blk_count * tok // SUB
    smem = pl.BlockSpec(memory_space=pltpu.SMEM)
    vmem = pl.BlockSpec(memory_space=pltpu.VMEM)
    hbm = pl.BlockSpec(memory_space=pl.ANY)
    tiles = pltpu.VMEM((chips, tok, q_cols), BF)
    thin = pltpu.VMEM((chips, CHUNKS, heads, tok), F32)
    dma = pltpu.SemaphoreType.DMA
    return pl.pallas_call(
        functools.partial(kernel, chips, depth),
        out_shape=jax.ShapeDtypeStruct((tok, out_cols), BF),
        in_specs=[smem] * 3 + [vmem] * 3 + [hbm] * 3,
        out_specs=vmem,
        scratch_shapes=[
            pltpu.SMEM((subs,), jnp.int32),
            pltpu.SMEM((subs,), jnp.int32),
            pltpu.SMEM((subs,), jnp.int32),
            pltpu.SMEM((blocks,), jnp.int32),
            pltpu.VMEM(prefix_block_keys.shape, BF),
            pltpu.VMEM(prefix_block_values.shape, BF),
            pltpu.VMEM(w_out.shape, BF),
            pltpu.VMEM((tok, kv_cols), BF),
            pltpu.VMEM((tok, kv_cols), BF),
            tiles,
            tiles,
            tiles,
            tiles,
            tiles,
            tiles,
            tiles,
            pltpu.VMEM((tok, q_cols), F32),
            pltpu.VMEM((chips, tok, HEAD_SIZE), F32),
            pltpu.VMEM((tok, HEAD_SIZE), F32),
            thin,
            thin,
            thin,
            thin,
            pltpu.VMEM((tok, HEAD_SIZE), F32),
            pltpu.VMEM((tok, q_cols), BF),
            pltpu.VMEM((depth, tok, out_cols), BF),
            pltpu.VMEM((depth, tok, out_cols), BF),
            dma((3,)),
            dma((4,)),
            dma((2, chips, CHUNKS)),
            dma((2, chips, CHUNKS)),
            dma((4, chips, CHUNKS)),
            dma((4, chips, CHUNKS)),
            dma((2, depth, CHUNKS)),
        ],
        compiler_params=pltpu.CompilerParams(
            collective_id=0, has_side_effects=True, vmem_limit_bytes=56 * 1024 * 1024
        ),
    )(
        suffix_len,
        request_group,
        block_group,
        queries,
        suffix_key_rows,
        suffix_value_rows,
        prefix_block_keys,
        prefix_block_values,
        w_out,
    )


def solution(mesh):
    placed = (
        P("blk", "kvh"),
        P("blk", "kvh"),
        P("blk", "kvh"),
        P("blk", None, "kvh"),
        P("blk", None, "kvh"),
        P("blk"),
        P(),
        P(),
        P("kvh", None),
    )
    return jax.shard_map(
        per_device, mesh=mesh, in_specs=placed, out_specs=P("blk", "kvh"), check_vma=False
    )
```
